256 devices in a mesh: dp: 16 (over x_hi, y, core), tensor: 16 (over z, x_lo).
Axes of the slice: x: 4 (x_hi: 2, x_lo: 2; x = x_hi * 2 + x_lo), y: 4, z: 8, core: 2. Of those that a mesh axis runs over, the one named last changes fastest.
Arguments:
- activations: bfloat16 [2048, 4096], P(('dp', 'tensor')), may hold values from -24 to 24
- gate_pre: bfloat16 [2048, 14336], P('dp', 'tensor'), may hold values from -6 to 6
- up_pre: bfloat16 [2048, 14336], P('dp', 'tensor'), may hold values from -6 to 6
- hidden_grad: bfloat16 [2048, 14336], P('dp', 'tensor'), may hold values from -6 to 6
- gate_weight: bfloat16 [4096, 14336], P('dp', 'tensor'), may hold values from -0.09375 to 0.09375
- up_weight: bfloat16 [4096, 14336], P('dp', 'tensor'), may hold values from -0.09375 to 0.09375
Outputs:
- input_grad: bfloat16 [2048, 4096], P(('dp', 'tensor'))
- gate_weight_grad: bfloat16 [4096, 14336], P('dp', 'tensor')
- up_weight_grad: bfloat16 [4096, 14336], P('dp', 'tensor')
The draws below stay inside these ranges and needn't reach their ends.
All inputs are finite; a program needn't handle non-finite values.
Results may differ from the reference program's by a relative error of at most 0.024.
Values may be sent and summed in bfloat16 or wider, within the bound.
A program may use at most 128 MiB of HBM per device.

```python
import jax
import jax.numpy as jnp
from jax import lax

D = 4096
FF = 14336
TOK_DP = 128
TOKENS = 2048
N_DP = 16
N_TENSOR = 16


def strengthened(result, rng, source, target, parts, factor):
    owner, partner = [(jnp.arange(result.shape[dim]) // (result.shape[dim] // parts)).reshape([-1 if axis == dim else 1 for axis in range(result.ndim)]) for dim in (source, target)]
    chosen = jax.random.permutation(rng, parts)[partner]
    strong = (owner == chosen) | (owner == (partner + parts // 2) % parts)
    return jnp.where(strong, factor * result, result)


def levels(rng, shape, pieces, low, largest):
    gain = 1.0
    for axis_at, blocks in pieces:
        heights = jax.random.uniform(jax.random.fold_in(jax.random.fold_in(rng, 6), axis_at), (blocks,), jnp.float32, low / len(pieces), largest / len(pieces))
        gain = gain * jnp.repeat(jnp.exp(heights), shape[axis_at] // blocks).reshape((-1,) + (1,) * (len(shape) - 1 - axis_at))
    return gain


def normal_values(own_key, shape, deviation, limit, pieces=(), held_as=jnp.bfloat16):
    values = jax.random.normal(own_key, shape, jnp.float32) * deviation
    if len(pieces) > 0:
        values = levels(own_key, shape, pieces, -0.22, 0.18) * values
    return jnp.clip(values, min=-limit, max=limit).astype(held_as)


def gaussian_with(rng, extent, scale, reach, cuts, heavy, kind=jnp.bfloat16):
    result = scale * jax.random.normal(rng, extent, jnp.float32)
    if cuts:
        result = result * levels(rng, extent, cuts, -0.22, 0.18)
    return jnp.clip(strengthened(result, jax.random.fold_in(rng, 3), *heavy), -reach, reach).astype(kind)


def setup_inputs(seed: int = 0) -> dict:
    key_list = jax.random.split(jax.random.key(seed), 7)
    return {
        "activations": gaussian_with(key_list[0], (TOKENS, D), 1.0, 24.0, ((0, 256),), (0, 1, 256, 6.0)),
        "gate_pre": normal_values(key_list[1], (TOKENS, FF), 1.0, 6.0, ((0, 16), (1, 16))),
        "up_pre": normal_values(key_list[2], (TOKENS, FF), 1.0, 6.0, ((0, 16), (1, 16))),
        "hidden_grad": gaussian_with(key_list[3], (TOKENS, FF), 1.0, 6.0, ((0, 16), (1, 16)), (1, 0, 16, 2.0)),
        "gate_weight": normal_values(key_list[4], (D, FF), D ** -0.5, 0.09375, ((0, 16), (1, 16))),
        "up_weight": normal_values(key_list[5], (D, FF), D ** -0.5, 0.09375, ((0, 16), (1, 16))),
    }


def reference(activations, gate_pre, up_pre, hidden_grad, gate_weight, up_weight):
    gate_value = gate_pre.astype(jnp.float32)
    up_value = up_pre.astype(jnp.float32)
    upstream = hidden_grad.astype(jnp.float32)
    gate_sigmoid = jax.nn.sigmoid(gate_value)
    grad_up = (upstream * gate_value * gate_sigmoid).astype(jnp.bfloat16)
    grad_gate = (upstream * up_value * gate_sigmoid * (1.0 + gate_value * (1.0 - gate_sigmoid))).astype(jnp.bfloat16)
    unit_block = FF // N_TENSOR
    gate_blocks = grad_gate.reshape(TOKENS, N_TENSOR, unit_block).transpose(1, 0, 2)
    up_blocks = grad_up.reshape(TOKENS, N_TENSOR, unit_block).transpose(1, 0, 2)
    wgate_blocks = gate_weight.reshape(D, N_TENSOR, unit_block).transpose(1, 0, 2)
    wup_blocks = up_weight.reshape(D, N_TENSOR, unit_block).transpose(1, 0, 2)

    def add_units(total, items):
        gate_block, up_block, wgate_block, wup_block = items
        dims = (((1,), (1,)), ((), ()))
        partial_sum = lax.dot_general(gate_block, wgate_block, dims, preferred_element_type=jnp.float32)
        partial_sum = partial_sum + lax.dot_general(up_block, wup_block, dims, preferred_element_type=jnp.float32)
        rounded = lax.optimization_barrier(partial_sum.astype(jnp.bfloat16))
        return total + rounded.astype(jnp.float32), None

    input_total, _ = lax.scan(add_units, jnp.zeros((TOKENS, D), jnp.float32), (gate_blocks, up_blocks, wgate_blocks, wup_blocks))
    input_grad = input_total.astype(jnp.bfloat16)

    grad_scale = float(TOKENS) ** -0.5
    both_grads = jnp.concatenate((grad_gate, grad_up), axis=1).reshape(N_DP, TOK_DP, 2 * FF)
    feature_blocks = activations.reshape(N_DP, TOK_DP, D)

    def add_tokens(total, items):
        feature_block, grad_block = items
        partial_sum = lax.dot_general(feature_block, grad_block, (((0,), (0,)), ((), ())), preferred_element_type=jnp.float32) * grad_scale
        rounded = lax.optimization_barrier(partial_sum.astype(jnp.bfloat16))
        return total + rounded.astype(jnp.float32), None

    weight_total, _ = lax.scan(add_tokens, jnp.zeros((D, 2 * FF), jnp.float32), (feature_blocks, both_grads))
    weight_grads = weight_total.astype(jnp.bfloat16)
    return input_grad, weight_grads[:, :FF], weight_grads[:, FF:]
```

```python
import jax
import jax.numpy as jnp
from jax import lax
from jax.sharding import PartitionSpec as P


def body(activations, gate_pre, up_pre, hidden_grad, gate_weight, up_weight):
    n_dp = lax.axis_size("dp")
    n_tensor = lax.axis_size("tensor")
    own_tokens, model = activations.shape
    rows, width = gate_weight.shape
    group_tokens = gate_pre.shape[0]
    gate_value = gate_pre.astype(jnp.float32)
    up_value = up_pre.astype(jnp.float32)
    upstream = hidden_grad.astype(jnp.float32)
    gate_sigmoid = jax.nn.sigmoid(gate_value)
    grad_up = (upstream * gate_value * gate_sigmoid).astype(jnp.bfloat16)
    grad_gate = (
        upstream * up_value * gate_sigmoid * (1.0 + gate_value * (1.0 - gate_sigmoid))
    ).astype(jnp.bfloat16)
    own_grads = jnp.concatenate((grad_gate, grad_up), axis=1)
    both_weights = jnp.concatenate((gate_weight, up_weight), axis=1)
    all_grads = lax.all_gather(own_grads, "dp", axis=0, tiled=False)

    pieces = activations.reshape(own_tokens, n_dp, rows).transpose(1, 0, 2)
    pieces = lax.all_to_all(pieces, "dp", split_axis=0, concat_axis=0, tiled=True)
    features = lax.all_gather(pieces, "tensor", axis=1, tiled=True)

    terms = lax.dot_general(
        all_grads.reshape(n_dp * group_tokens, 2 * width), both_weights,
        (((1,), (1,)), ((), ())), preferred_element_type=jnp.float32,
    ).astype(jnp.bfloat16)
    terms = terms.reshape(n_dp, n_tensor, own_tokens, rows).transpose(1, 0, 2, 3)
    terms = terms.reshape(n_dp * group_tokens, rows)
    summed = lax.psum_scatter(terms, "tensor", scatter_dimension=0, tiled=True)
    summed = summed.reshape(n_dp, own_tokens, rows)
    input_grad = lax.all_to_all(summed, "dp", split_axis=0, concat_axis=0, tiled=True)
    input_grad = input_grad.transpose(1, 0, 2).reshape(own_tokens, model)

    grad_scale = float(group_tokens * n_dp) ** (-0.5)
    weight_grad = (
        lax.dot_general(
            features.reshape(n_dp * group_tokens, rows), all_grads.reshape(n_dp * group_tokens, 2 * width),
            (((0,), (0,)), ((), ())), preferred_element_type=jnp.float32,
        ) * grad_scale
    ).astype(jnp.bfloat16)
    return (input_grad, weight_grad[:, :width], weight_grad[:, width:])


def solution(mesh):
    in_specs = (
        P(("dp", "tensor"), None),
        P("dp", "tensor"),
        P("dp", "tensor"),
        P("dp", "tensor"),
        P("dp", "tensor"),
        P("dp", "tensor"),
    )
    out_specs = (P(("dp", "tensor"), None), P("dp", "tensor"), P("dp", "tensor"))
    return jax.shard_map(body, mesh=mesh, in_specs=in_specs, out_specs=out_specs, check_vma=False)
```

```python
import functools

import jax
import jax.numpy as jnp
from jax import lax
from jax.experimental import pallas as pl
from jax.experimental.pallas import tpu as pltpu
from jax.sharding import PartitionSpec as P

MESH = pl.DeviceIdType.MESH
BF16, F32 = jnp.bfloat16, jnp.float32
CHUNKS = ((0, 0), (1, 0), (0, 1), (0, 3), (0, 2), (1, 1), (1, 3), (1, 2))
SLOT = {chunk: at for at, chunk in enumerate(CHUNKS)}
PARTS = 4
N_COPIES = 192


def kernel(
    grad_scale,
    act_hbm, gate_hbm, up_hbm, hidden_hbm, wgate_hbm, wup_hbm,
    igrad_ref, ggrad_hbm, ugrad_hbm,
    act, gate, up, hidden, weights, weights_t, grads,
    a_send, a_recv, a_mine, a_other, a_all, a_t, total, out_buf,
    p_send, p_recv, p_own, z_send, z_recv, f_send, f_recv,
    send_sems, recv_sems, local_sems,
):
    dp, tensor = lax.axis_index("dp"), lax.axis_index("tensor")
    x_hi, y, core = dp // 8, (dp // 2) % 4, dp % 2
    z, x_lo = tensor // 2, tensor % 2
    width = gate.shape[1]

    def dp_peer(rx, ry, rc):
        index = (((x_hi + rx) % 2) * 4 + (y + ry) % 4) * 2 + (core + rc) % 2
        return {"dp": index, "tensor": tensor}, index

    def z_peer(to):
        return {"dp": dp, "tensor": to * 2 + x_lo}

    x_peer = {"dp": dp, "tensor": z * 2 + 1 - x_lo}
    opposite = dp_peer(1, 0, 0)[0]
    above, below = dp_peer(0, 1, 0)[0], dp_peer(0, 3, 0)[0]
    twin = dp_peer(0, 0, 1)[0]

    copies = []

    def send(src, dst, peer):
        at = len(copies)
        copy = pltpu.make_async_remote_copy(
            src_ref=src, dst_ref=dst, send_sem=send_sems.at[at], recv_sem=recv_sems.at[at],
            device_id=peer, device_id_type=MESH,
        )
        copy.start()
        copies.append(copy)
        return copy

    local = []

    def load(src, dst):
        copy = pltpu.make_async_copy(src, dst, local_sems.at[len(local)])
        copy.start()
        local.append(copy)
        return copy

    def rows(j):
        return pl.ds(pl.multiple_of(((z // 2 + 1 + j) % PARTS) * 32, 32), 32)

    loads = []
    act_load = load(act_hbm, act)
    for j in range(PARTS):
        loads.append([load(src.at[rows(j)], dst.at[rows(j)]) for src, dst in (
            (gate_hbm, gate), (up_hbm, up), (hidden_hbm, hidden))])
    weight_loads = [load(wgate_hbm, weights.at[0]), load(wup_hbm, weights.at[1])]

    barrier = pltpu.get_barrier_semaphore()
    peers = [dp_peer(rx, ry, rc)[0] for rx, ry in CHUNKS for rc in range(2) if rx or ry or rc]
    peers += [z_peer((z + k) % 8) for k in range(1, 8)] + [x_peer]
    for peer in peers:
        pl.semaphore_signal(barrier, inc=1, device_id=peer, device_id_type=MESH)

    got = {}

    def send_part(chunk, j, peer, to_chunk, to_core=0):
        at = SLOT[chunk], 0, rows(j)
        return send(grads.at[at], grads.at[SLOT[to_chunk], to_core, rows(j)], peer)

    def to_twin(chunk, j):
        got[chunk, 1, j] = send_part(chunk, j, twin, chunk, 1)

    for j in range(PARTS):
        for copy in loads[j]:
            copy.wait()
        gate_value = gate[rows(j), :].astype(F32)
        up_value = up[rows(j), :].astype(F32)
        upstream = hidden[rows(j), :].astype(F32)
        gate_sigmoid = jax.nn.sigmoid(gate_value)
        scaled = upstream * gate_sigmoid
        grads[0, 0, rows(j), 0:width] = (
            scaled * up_value * (1.0 + gate_value * (1.0 - gate_sigmoid))
        ).astype(BF16)
        grads[0, 0, rows(j), width:2 * width] = (scaled * gate_value).astype(BF16)
        if j == 0:
            pl.semaphore_wait(barrier, len(peers))
        got[(1, 0), 0, j] = send_part((0, 0), j, opposite, (1, 0))
        got[(0, 3), 0, j] = send_part((0, 0), j, above, (0, 3))
        got[(0, 1), 0, j] = send_part((0, 0), j, below, (0, 1))
        to_twin((0, 0), j)

    act_load.wait()
    wide = act[...].astype(F32)
    for index in range(16):
        at = index * 256
        a_send[index] = jnp.concatenate(
            (wide[:, at:at + 128], wide[:, at + 128:at + 256]), axis=0
        ).astype(BF16)
    a_copies = []
    for rx, ry in CHUNKS:
        for rc in range(2):
            if rx or ry or rc:
                peer, index = dp_peer(rx, ry, rc)
                a_copies.append(send(a_send.at[index], a_recv.at[SLOT[rx, -ry % 4], rc], peer))
    a_recv[0, 0] = a_send[dp]

    for copy in weight_loads:
        copy.wait()
    for half in range(2):
        weights_t[half] = weights[half].astype(F32).T.astype(BF16)

    groups = {}

    def wait_parts(chunks, parts, cores=(0, 1)):
        for chunk in chunks:
            for j in parts:
                for rc in cores:
                    if (chunk, rc, j) in got:
                        got.pop((chunk, rc, j)).wait_recv()

    def ig_product(name, chunks, parts):
        first, n = SLOT[chunks[0]], len(chunks)
        base = ig_product.used
        ig_product.used += n * len(parts)
        for at, chunk in enumerate(chunks):
            lhs = jnp.concatenate(
                [grads[SLOT[chunk], rc, rows(j), :] for j in parts for rc in range(2)], axis=0
            )
            term = jnp.dot(lhs[:, :width], weights_t[0], preferred_element_type=F32)
            term += jnp.dot(lhs[:, width:], weights_t[1], preferred_element_type=F32)
            term = term.reshape(len(parts), 2, 2, 2, 8, 256)
            low, high = term[:, :, :, 0], term[:, :, :, 1]
            own = jnp.where(x_lo == 0, low, high)
            other = jnp.where(x_lo == 0, high, low)
            for i in range(len(parts)):
                unit = base + at * len(parts) + i
                for e in range(2):
                    p_own[unit, e] = jnp.concatenate((own[i, 0, e], own[i, 1, e]), axis=0)
                    p_send[unit, e] = jnp.concatenate((other[i, 0, e], other[i, 1, e]), axis=0).astype(BF16)
        units = pl.ds(base, n * len(parts))
        groups[name] = (send(p_send.at[units], p_recv.at[units], x_peer), chunks, parts, base)

    ig_product.used = 0
    z_copies = {}

    def ig_pair(name):
        copy, chunks, parts, base = groups.pop(name)
        first, n = SLOT[chunks[0]], len(chunks)
        copy.wait_recv()
        for at in range(n):
            for i, j in enumerate(parts):
                unit = base + at * len(parts) + i
                z_send[j, :, first + at] = (p_own[unit] + p_recv[unit].astype(F32)).astype(BF16)
        for j in parts:
            for r in range(2):
                if j == PARTS - 1 and r == 0:
                    continue
                e = (z + r) % 2
                to = ((z // 2 + 1 + j) % 4) * 2 + e
                z_copies.setdefault(chunks, []).append(send(
                    z_send.at[j, e, pl.ds(first, n)], z_recv.at[j, r, pl.ds(first, n)], z_peer(to)))

    f_copies = []

    def ig_final(chunks):
        first, n = SLOT[chunks[0]], len(chunks)
        for copy in z_copies.pop(chunks):
            copy.wait_recv()
        for at, (rx, ry) in enumerate(chunks):
            total_z = z_send[PARTS - 1, z % 2, first + at].astype(F32)
            for j in range(PARTS):
                for r in range(2):
                    if j < PARTS - 1 or r:
                        total_z += z_recv[j, r, first + at].astype(F32)
            back = rx * 4 + -ry % 4
            for rc in range(2):
                if rx or ry or rc:
                    f_send[first + at, rc] = total_z[rc * 8:rc * 8 + 8]
                    f_copies.append(send(f_send.at[first + at, rc], f_recv.at[back, rc], dp_peer(rx, ry, rc)[0]))
                else:
                    f_recv[0, 0] = total_z[0:8]

    wait_parts([(0, 0)], range(PARTS))
    ig_product("own", ((0, 0),), range(PARTS))

    for copy in a_copies:
        copy.wait_recv()
    pieces = a_recv[...].astype(F32).reshape(16, 2, 8, 128)
    pieces = jnp.concatenate((pieces[:, 0], pieces[:, 1]), axis=-1)
    a_mine[...] = pieces.reshape(128, 256).astype(BF16)
    a_pair = send(a_mine, a_other, x_peer)

    def forward_own_row(j):
        wait_parts([(1, 0)], [j], (0,))
        got[(1, 3), 0, j] = send_part((1, 0), j, above, (1, 3))
        got[(1, 1), 0, j] = send_part((1, 0), j, below, (1, 1))
        to_twin((1, 0), j)
        wait_parts([(0, 3), (0, 1)], [j], (0,))
        if j % 2 == 0:
            got[(0, 2), 0, j] = send_part((0, 3), j, above, (0, 2))
        else:
            got[(0, 2), 0, j] = send_part((0, 1), j, below, (0, 2))
        to_twin((0, 3), j)
        to_twin((0, 1), j)

    ring = {}

    def ring_step(step):
        right, left = z_peer((z + 1) % 8), z_peer((z + 7) % 8)
        if step:
            ring["right"].wait_recv()
            ring["left"].wait_recv()
        up_block, down_block = (z + 8 - step) % 8, (z + step) % 8
        if step < 3:
            ring["right"] = send(a_all.at[up_block], a_all.at[up_block], right)
            ring["left"] = send(a_all.at[down_block], a_all.at[down_block], left)
        elif step == 3:
            ring["right"] = send(a_all.at[up_block, pl.ds(0, 4)], a_all.at[up_block, pl.ds(0, 4)], right)
            ring["left"] = send(a_all.at[down_block, pl.ds(4, 4)], a_all.at[down_block, pl.ds(4, 4)], left)

    forward_own_row(0)
    a_pair.wait_recv()
    mine = a_mine[...].astype(F32).reshape(16, 8, 256)
    other = a_other[...].astype(F32).reshape(16, 8, 256)
    both = jnp.stack((jnp.where(x_lo == 0, mine, other), jnp.where(x_lo == 0, other, mine)), axis=1)
    a_all[z] = both.reshape(8, 2, 16, 256).astype(BF16)
    ring_step(0)
    ig_pair("own")
    forward_own_row(1)
    ring_step(1)
    forward_own_row(2)
    ring_step(2)
    forward_own_row(3)

    early = ((1, 0), (0, 1), (0, 3))
    wait_parts(early, range(PARTS))
    ig_product("early", early, range(PARTS))
    ring_step(3)
    ig_final(((0, 0),))
    for j in range(PARTS):
        wait_parts([(0, 2)], [j], (0,))
        to_twin((0, 2), j)
    ig_pair("early")

    def forward_other_row(j):
        wait_parts([(1, 3), (1, 1)], [j], (0,))
        if j % 2 == 0:
            got[(1, 2), 0, j] = send_part((1, 3), j, above, (1, 2))
        else:
            got[(1, 2), 0, j] = send_part((1, 1), j, below, (1, 2))
        to_twin((1, 3), j)
        to_twin((1, 1), j)

    forward_other_row(0)
    wait_parts([(0, 2)], range(PARTS))
    ig_product("across", ((0, 2),), range(PARTS))
    ring_step(4)
    for at in range(8):
        block = jnp.concatenate([a_all[zz, at, rc] for rc in range(2) for zz in range(8)], axis=0)
        a_t[:, at * 256:(at + 1) * 256] = block.astype(F32).T.astype(BF16)
    forward_other_row(1)
    late = ((1, 1), (1, 3))
    wait_parts(late, (0, 1))
    ig_product("late0", late, (0, 1))
    ig_pair("across")
    ig_final(early)
    for half in range(2):
        cols = slice(half * width, (half + 1) * width)
        total[:, cols] = jnp.dot(
            a_t[:, 0:1280], grads[0:5, :, :, cols].reshape(1280, width), preferred_element_type=F32)
    forward_other_row(2)
    forward_other_row(3)
    ig_pair("late0")
    wait_parts(late, (2, 3))
    ig_product("late1", late, (2, 3))
    ig_final(((0, 2),))
    for j in range(PARTS):
        wait_parts([(1, 2)], [j], (0,))
        to_twin((1, 2), j)
    ig_pair("late1")
    wait_parts([(1, 2)], range(PARTS))
    ig_product("last", ((1, 2),), range(PARTS))
    outs = []
    for half, out_hbm in enumerate((ggrad_hbm, ugrad_hbm)):
        cols = slice(half * width, (half + 1) * width)
        out_buf[half] = ((total[:, cols] + jnp.dot(
            a_t[:, 1280:2048], grads[5:8, :, :, cols].reshape(768, width), preferred_element_type=F32)
        ) * grad_scale).astype(BF16)
        outs.append(load(out_buf.at[half], out_hbm))
        if half == 0:
            ig_pair("last")
    ig_final(late)
    ig_final(((1, 2),))
    for copy in f_copies:
        copy.wait_recv()
    for index in range(16):
        rel = ((index // 8 + x_hi) % 2) * 4 + (index // 2 % 4 - y + 4) % 4
        igrad_ref[:, index * 256:(index + 1) * 256] = f_recv[rel, (index % 2 + core) % 2].astype(BF16)
    for copy in outs:
        copy.wait()
    for copy in copies:
        copy.wait_send()


def body(*args):
    activations, gate_pre, _, _, gate_weight, _ = args
    own_tokens, model = activations.shape
    rows, width = gate_weight.shape
    tokens = gate_pre.shape[0]
    n_dp = lax.axis_size("dp")
    any_spec = pl.BlockSpec(memory_space=pl.ANY)
    return pl.pallas_call(
        functools.partial(kernel, float(tokens * n_dp) ** (-0.5)),
        out_shape=(
            jax.ShapeDtypeStruct((own_tokens, model), BF16),
            jax.ShapeDtypeStruct((rows, width), BF16),
            jax.ShapeDtypeStruct((rows, width), BF16),
        ),
        in_specs=[any_spec] * 6,
        out_specs=(pl.BlockSpec(memory_space=pltpu.VMEM), any_spec, any_spec),
        scratch_shapes=[
            pltpu.VMEM((own_tokens, model), BF16),
            pltpu.VMEM((tokens, width), BF16),
            pltpu.VMEM((tokens, width), BF16),
            pltpu.VMEM((tokens, width), BF16),
            pltpu.VMEM((2, rows, width), BF16),
            pltpu.VMEM((2, width, rows), BF16),
            pltpu.VMEM((8, 2, tokens, 2 * width), BF16),
            pltpu.VMEM((16, 16, 128), BF16),
            pltpu.VMEM((8, 2, 16, 128), BF16),
            pltpu.VMEM((128, 256), BF16),
            pltpu.VMEM((128, 256), BF16),
            pltpu.VMEM((8, 8, 2, 16, 256), BF16),
            pltpu.VMEM((rows, tokens * n_dp), BF16),
            pltpu.VMEM((rows, 2 * width), F32),
            pltpu.VMEM((2, rows, width), BF16),
            pltpu.VMEM((32, 2, 16, 256), BF16),
            pltpu.VMEM((32, 2, 16, 256), BF16),
            pltpu.VMEM((32, 2, 16, 256), F32),
            pltpu.VMEM((PARTS, 2, 8, 16, 256), BF16),
            pltpu.VMEM((PARTS, 2, 8, 16, 256), BF16),
            pltpu.VMEM((8, 2, 8, 256), F32),
            pltpu.VMEM((8, 2, 8, 256), F32),
            pltpu.SemaphoreType.DMA((N_COPIES,)),
            pltpu.SemaphoreType.DMA((N_COPIES,)),
            pltpu.SemaphoreType.DMA((32,)),
        ],
        compiler_params=pltpu.CompilerParams(
            collective_id=0, has_side_effects=True, vmem_limit_bytes=48 * 2**20
        ),
        cost_estimate=pl.CostEstimate(flops=3_758_096_384, bytes_accessed=4_500_000, transcendentals=114_688),
    )(*args)


def solution(mesh):
    in_specs = (
        P(("dp", "tensor"), None),
        P("dp", "tensor"),
        P("dp", "tensor"),
        P("dp", "tensor"),
        P("dp", "tensor"),
        P("dp", "tensor"),
    )
    out_specs = (P(("dp", "tensor"), None), P("dp", "tensor"), P("dp", "tensor"))
    return jax.shard_map(body, mesh=mesh, in_specs=in_specs, out_specs=out_specs, check_vma=False)
```

```python
import functools

import jax
import jax.numpy as jnp
from jax import lax
from jax.experimental import pallas as pl
from jax.experimental.pallas import tpu as pltpu
from jax.sharding import PartitionSpec as P

MESH = pl.DeviceIdType.MESH
BF16, F32 = jnp.bfloat16, jnp.float32
CHUNKS = ((0, 0), (1, 0), (0, 1), (0, 3), (0, 2), (1, 1), (1, 3), (1, 2))
SLOT = {chunk: at for at, chunk in enumerate(CHUNKS)}
PARTS = 4
N_COPIES = 96


def kernel(
    grad_scale,
    act_hbm, gate_hbm, up_hbm, hidden_hbm, wgate_hbm, wup_hbm,
    igrad_ref, ggrad_ref, ugrad_ref,
    act, gate, up, hidden, weights, weights_t, grads,
    a_send, a_got, a_all, a_t, total,
    p_send, p_recv, p_own, p_out, z_send, z_recv, f_send, f_recv,
    send_sems, recv_sems, local_sems,
):
    dp, tensor = lax.axis_index("dp"), lax.axis_index("tensor")
    x_hi, y, core = dp // 8, (dp // 2) % 4, dp % 2
    z, x_lo = tensor // 2, tensor % 2
    width = gate.shape[1]

    def dp_peer(rx, ry, rc):
        index = (((x_hi + rx) % 2) * 4 + (y + ry) % 4) * 2 + (core + rc) % 2
        return {"dp": index, "tensor": tensor}, index

    def z_peer(to):
        return {"dp": dp, "tensor": to * 2 + x_lo}

    x_peer = {"dp": dp, "tensor": z * 2 + 1 - x_lo}
    opposite = dp_peer(1, 0, 0)[0]
    above, below = dp_peer(0, 1, 0)[0], dp_peer(0, 3, 0)[0]
    twin = dp_peer(0, 0, 1)[0]

    copies = []

    def send(src, dst, peer):
        at = len(copies)
        copy = pltpu.make_async_remote_copy(
            src_ref=src, dst_ref=dst, send_sem=send_sems.at[at], recv_sem=recv_sems.at[at],
            device_id=peer, device_id_type=MESH,
        )
        copy.start()
        copies.append(copy)
        return copy

    local = []

    def load(src, dst):
        copy = pltpu.make_async_copy(src, dst, local_sems.at[len(local)])
        copy.start()
        local.append(copy)
        return copy

    def rows(j):
        return pl.ds(pl.multiple_of(((z // 2 + 1 + j) % PARTS) * 32, 32), 32)

    loads = []
    act_load = load(act_hbm, act.at[0])
    for j in range(PARTS):
        loads.append([load(src.at[rows(j)], dst.at[rows(j)]) for src, dst in (
            (gate_hbm, gate), (up_hbm, up), (hidden_hbm, hidden))])
    weight_loads = [load(wgate_hbm, weights.at[0]), load(wup_hbm, weights.at[1])]

    barrier = pltpu.get_barrier_semaphore()
    peers = [dp_peer(rx, ry, 0)[0] for rx, ry in CHUNKS[1:]] + [twin]
    peers += [z_peer((z + k) % 8) for k in range(1, 8)] + [x_peer]
    for peer in peers:
        pl.semaphore_signal(barrier, inc=1, device_id=peer, device_id_type=MESH)

    got = {}
    a_pairs = []

    def send_part(chunk, j, peer, to_chunk):
        at = rows(j)
        got[to_chunk, j] = send(grads.at[SLOT[chunk], 0, at], grads.at[SLOT[to_chunk], 0, at], peer)

    def to_twin(chunk):
        got["twin", chunk] = send(grads.at[SLOT[chunk], 0], grads.at[SLOT[chunk], 1], twin)

    def wait_parts(chunks, parts):
        for chunk in chunks:
            for j in parts:
                if (chunk, j) in got:
                    got.pop((chunk, j)).wait_recv()

    def own_part(j):
        for copy in loads[j]:
            copy.wait()
        gate_value = gate[rows(j), :].astype(F32)
        up_value = up[rows(j), :].astype(F32)
        upstream = hidden[rows(j), :].astype(F32)
        gate_sigmoid = jax.nn.sigmoid(gate_value)
        scaled = upstream * gate_sigmoid
        grads[0, 0, rows(j), 0:width] = (
            scaled * up_value * (1.0 + gate_value * (1.0 - gate_sigmoid))
        ).astype(BF16)
        grads[0, 0, rows(j), width:2 * width] = (scaled * gate_value).astype(BF16)
        if j == 0:
            pl.semaphore_wait(barrier, len(peers))
            act_load.wait()
            a_pairs.append(send(act.at[0], act.at[1], x_peer))
        send_part((0, 0), j, above, (0, 3))
        send_part((0, 0), j, below, (0, 1))
        send_part((0, 0), j, opposite, (1, 0))

    own_part(0)
    own_part(1)
    a_pairs[0].wait_recv()
    mine, other = act[0].astype(F32), act[1].astype(F32)
    both = jnp.concatenate((jnp.where(x_lo == 0, mine, other), jnp.where(x_lo == 0, other, mine)), axis=0)
    for chip in range(8):
        for rc in range(2):
            at = (chip * 2 + rc) * 256
            a_send[chip, (rc + core) % 2] = both[:, at:at + 256].astype(BF16)
    a_copies = []
    for rx, ry in CHUNKS[1:]:
        peer, index = dp_peer(rx, ry, 0)
        a_copies.append(send(a_send.at[index // 2], a_got.at[SLOT[rx, -ry % 4]], peer))
    a_got[0] = a_send[dp // 2]
    for j in range(2, PARTS):
        own_part(j)
    to_twin((0, 0))
    for copy in weight_loads:
        copy.wait()
    for half in range(2):
        weights_t[0, half] = weights[half].astype(F32).T.astype(BF16)
    w_copy = send(weights_t.at[0], weights_t.at[1], twin)

    def ig_product(units, base):
        for first in range(0, len(units), 8):
            some = units[first:first + 8]
            wait_parts_of(some)
            lhs = jnp.concatenate([grads[SLOT[chunk], 0, rows(j), :] for chunk, j in some], axis=0)
            at = pl.ds(base + first, len(some))
            for rc in range(2):
                term = jnp.dot(lhs[:, :width], weights_t[rc, 0], preferred_element_type=F32)
                term += jnp.dot(lhs[:, width:], weights_t[rc, 1], preferred_element_type=F32)
                term = term.reshape(len(some), 2, 2, 8, 256)
                low, high = term[:, :, 0], term[:, :, 1]
                here = at, slice(None), pl.ds(rc * 8, 8)
                p_own[here] = jnp.where(x_lo == 0, low, high)
                p_out[here] = jnp.where(x_lo == 0, high, low)
            p_send[at] = p_out[at].astype(BF16)

    def wait_parts_of(units):
        for chunk, j in units:
            wait_parts([chunk], [j])

    def ig_exchange(base, n):
        at = pl.ds(base, n)
        return send(p_send.at[at], p_recv.at[at], x_peer)

    z_copies = {}

    def ig_pair(copy, units, base, spans):
        copy.wait_recv()
        for at, (chunk, j) in enumerate(units):
            z_send[j, :, SLOT[chunk]] = (p_own[base + at] + p_recv[base + at].astype(F32)).astype(BF16)
        for first, n, parts in spans:
            for j in parts:
                for r in range(2):
                    if j == PARTS - 1 and r == 0:
                        continue
                    e = (z + r) % 2
                    to = ((z // 2 + 1 + j) % 4) * 2 + e
                    at = pl.ds(first, n)
                    z_copies.setdefault(first, []).append(
                        send(z_send.at[j, e, at], z_recv.at[j, r, at], z_peer(to)))

    f_copies = []

    def ig_final(chunks):
        first = SLOT[chunks[0]]
        for copy in z_copies.pop(first):
            copy.wait_recv()
        for at, (rx, ry) in enumerate(chunks):
            total_z = z_send[PARTS - 1, z % 2, first + at].astype(F32)
            for j in range(PARTS):
                for r in range(2):
                    if j < PARTS - 1 or r:
                        total_z += z_recv[j, r, first + at].astype(F32)
            if rx or ry:
                f_send[first + at] = total_z
                back = rx * 4 + -ry % 4
                f_copies.append(send(f_send.at[first + at], f_recv.at[back], dp_peer(rx, ry, 0)[0]))
            else:
                f_recv[0] = total_z

    every = range(PARTS)

    def own_row(j):
        wait_parts([(0, 3), (0, 1)], [j])
        if j % 2 == 0:
            send_part((0, 3), j, above, (0, 2))
        wait_parts([(1, 0)], [j])
        send_part((1, 0), j, above, (1, 3))
        send_part((1, 0), j, below, (1, 1))
        if j % 2 == 1:
            send_part((0, 1), j, below, (0, 2))

    ring = {}

    def ring_step(step):
        right, left = z_peer((z + 1) % 8), z_peer((z + 7) % 8)
        if step:
            ring["right"].wait_recv()
            ring["left"].wait_recv()
        else:
            a_twin.wait_recv()
        up_block, down_block = (z + 8 - step) % 8, (z + step) % 8
        if step < 3:
            ring["right"] = send(a_all.at[up_block], a_all.at[up_block], right)
            ring["left"] = send(a_all.at[down_block], a_all.at[down_block], left)
        elif step == 3:
            ring["right"] = send(a_all.at[up_block, pl.ds(0, 4)], a_all.at[up_block, pl.ds(0, 4)], right)
            ring["left"] = send(a_all.at[down_block, pl.ds(4, 4)], a_all.at[down_block, pl.ds(4, 4)], left)

    def a_turn(at):
        block = jnp.concatenate([a_all[zz, at, rc] for rc in range(2) for zz in range(8)], axis=0)
        a_t[:, at * 256:(at + 1) * 256] = block.astype(F32).T.astype(BF16)

    sent = [0]

    def drain():
        for copy in copies[sent[0]:]:
            copy.wait_send()
        sent[0] = len(copies)

    own_row(0)
    w_copy.wait_recv()
    for copy in a_copies:
        copy.wait_recv()
    a_all[z, :, 0] = a_got[:, 0]
    a_twin = send(a_got.at[:, 1], a_all.at[z, :, 1], twin)
    own_row(1)
    near = [(chunk, j) for chunk in CHUNKS[:4] for j in every]
    ig_product(near[:4], 0)
    own_row(2)
    ring_step(0)
    own_row(3)
    for chunk in CHUNKS[1:4]:
        to_twin(chunk)
    ig_product(near[4:], 4)
    near_copy = ig_exchange(0, 16)
    ring_step(1)
    for j in range(2):
        wait_parts([(0, 2)], [j])
        send_part((0, 2), j, opposite, (1, 2))
    ig_pair(near_copy, near, 0, [(0, 4, every)])
    middle = [(chunk, j) for chunk in CHUNKS[4:7] for j in range(2)]
    ig_product(middle, 16)
    middle_copy = ig_exchange(16, 6)
    ring_step(2)
    wait_parts([(1, 3)], [2])
    send_part((1, 3), 2, above, (1, 2))
    ring_step(3)
    ig_pair(middle_copy, middle, 16, [(4, 3, range(2))])
    wait_parts([(1, 1)], [3])
    send_part((1, 1), 3, below, (1, 2))
    wait_parts(CHUNKS[4:7], every)
    for chunk in CHUNKS[4:7]:
        to_twin(chunk)
    far = [(chunk, j) for chunk in CHUNKS[4:7] for j in range(2, 4)] + [((1, 2), j) for j in range(2)]
    ig_product(far, 22)
    far_copy = ig_exchange(22, 8)
    ig_final(CHUNKS[:4])
    ring_step(4)
    for at in range(8):
        a_turn(at)
    last = [((1, 2), j) for j in range(2, 4)]
    ig_product(last, 30)
    last_copy = ig_exchange(30, 2)
    to_twin((1, 2))
    ig_pair(far_copy, far, 22, [(4, 3, range(2, 4)), (7, 1, range(2))])
    for chunk in CHUNKS[:5]:
        got.pop(("twin", chunk)).wait_recv()
    for half in range(2):
        cols = slice(half * width, (half + 1) * width)
        total[:, cols] = jnp.dot(
            a_t[:, 0:1280], grads[0:5, :, :, cols].reshape(1280, width), preferred_element_type=F32)
    ig_pair(last_copy, last, 30, [(7, 1, range(2, 4))])
    ig_final(CHUNKS[4:7])
    for chunk in CHUNKS[5:]:
        got.pop(("twin", chunk)).wait_recv()
    for half, out_ref in enumerate((ggrad_ref, ugrad_ref)):
        cols = slice(half * width, (half + 1) * width)
        out_ref[...] = ((total[:, cols] + jnp.dot(
            a_t[:, 1280:2048], grads[5:8, :, :, cols].reshape(768, width), preferred_element_type=F32)
        ) * grad_scale).astype(BF16)
        if half == 0:
            ig_final(CHUNKS[7:])
    drain()
    assert not got
    for copy in f_copies:
        copy.wait_recv()
    for index in range(16):
        rel = ((index // 8 + x_hi) % 2) * 4 + (index // 2 % 4 - y + 4) % 4
        at = pl.ds(pl.multiple_of(((index % 2 + core) % 2) * 8, 8), 8)
        igrad_ref[:, index * 256:(index + 1) * 256] = f_recv[rel, at].astype(BF16)


def body(*args):
    activations, gate_pre, _, _, gate_weight, _ = args
    own_tokens, model = activations.shape
    rows, width = gate_weight.shape
    tokens = gate_pre.shape[0]
    n_dp = lax.axis_size("dp")
    hbm, vmem = pl.BlockSpec(memory_space=pltpu.HBM), pl.BlockSpec(memory_space=pltpu.VMEM)
    results = pl.pallas_call(
        functools.partial(kernel, float(tokens * n_dp) ** (-0.5)),
        out_shape=(
            jax.ShapeDtypeStruct((own_tokens, model), BF16),
            jax.ShapeDtypeStruct((rows, width), BF16),
            jax.ShapeDtypeStruct((rows, width), BF16),
        ),
        in_specs=[hbm] * 6,
        out_specs=(vmem, vmem, vmem),
        scratch_shapes=[
            pltpu.VMEM((2, own_tokens, model), BF16),
            pltpu.VMEM((tokens, width), BF16),
            pltpu.VMEM((tokens, width), BF16),
            pltpu.VMEM((tokens, width), BF16),
            pltpu.VMEM((2, rows, width), BF16),
            pltpu.VMEM((2, 2, width, rows), BF16),
            pltpu.VMEM((8, 2, tokens, 2 * width), BF16),
            pltpu.VMEM((8, 2, 16, 256), BF16),
            pltpu.VMEM((8, 2, 16, 256), BF16),
            pltpu.VMEM((8, 8, 2, 16, 256), BF16),
            pltpu.VMEM((rows, tokens * n_dp), BF16),
            pltpu.VMEM((rows, 2 * width), F32),
            pltpu.VMEM((32, 2, 16, 256), BF16),
            pltpu.VMEM((32, 2, 16, 256), BF16),
            pltpu.VMEM((32, 2, 16, 256), F32),
            pltpu.VMEM((32, 2, 16, 256), F32),
            pltpu.VMEM((PARTS, 2, 8, 16, 256), BF16),
            pltpu.VMEM((PARTS, 2, 8, 16, 256), BF16),
            pltpu.VMEM((8, 16, 256), F32),
            pltpu.VMEM((8, 16, 256), F32),
            pltpu.SemaphoreType.DMA((N_COPIES,)),
            pltpu.SemaphoreType.DMA((N_COPIES,)),
            pltpu.SemaphoreType.DMA((32,)),
        ],
        compiler_params=pltpu.CompilerParams(
            collective_id=0, has_side_effects=True, vmem_limit_bytes=62 * 2**20
        ),
        cost_estimate=pl.CostEstimate(flops=3_758_096_384, bytes_accessed=4_500_000, transcendentals=114_688),
    )(*args)
    return pl.pallas_call(
        place,
        out_shape=tuple(jax.ShapeDtypeStruct(r.shape, r.dtype) for r in results),
        in_specs=[hbm] * 3,
        out_specs=(hbm,) * 3,
        scratch_shapes=[pltpu.VMEM(r.shape, r.dtype) for r in results] + [pltpu.SemaphoreType.DMA((6,))],
    )(*results)


def place(a_in, b_in, c_in, a_out, b_out, c_out, a, b, c, sems):
    steps = ((b_in, b, b_out), (c_in, c, c_out), (a_in, a, a_out))
    copies = [pltpu.make_async_copy(src, mid, sems.at[at]) for at, (src, mid, _) in enumerate(steps)]
    for copy in copies:
        copy.start()
    outs = []
    for at, (_, mid, dst) in enumerate(steps):
        copies[at].wait()
        outs.append(pltpu.make_async_copy(mid, dst, sems.at[3 + at]))
        outs[at].start()
    for copy in outs:
        copy.wait()


def solution(mesh):
    in_specs = (
        P(("dp", "tensor"), None),
        P("dp", "tensor"),
        P("dp", "tensor"),
        P("dp", "tensor"),
        P("dp", "tensor"),
        P("dp", "tensor"),
    )
    out_specs = (P(("dp", "tensor"), None), P("dp", "tensor"), P("dp", "tensor"))
    return jax.shard_map(body, mesh=mesh, in_specs=in_specs, out_specs=out_specs, check_vma=False)
```

```python
import functools

import jax
import jax.numpy as jnp
from jax import lax
from jax.experimental import pallas as pl
from jax.experimental.pallas import tpu as pltpu
from jax.sharding import PartitionSpec as P

MESH = pl.DeviceIdType.MESH
BF16, F32 = jnp.bfloat16, jnp.float32
CHUNKS = ((0, 0), (1, 0), (0, 2), (1, 1), (1, 3), (1, 2), (0, 1), (0, 3))
SLOT = {chunk: at for at, chunk in enumerate(CHUNKS)}
PARTS = 4
N_COPIES = 112


def kernel(
    grad_scale,
    act_hbm, gate_hbm, up_hbm, hidden_hbm, wgate_hbm, wup_hbm,
    igrad_hbm, ggrad_hbm, ugrad_hbm,
    act, gate, up, hidden, weights, weights_t, grads,
    a_send, a_got, a_all, a_t, total, out_buf, igrad,
    p_send, p_recv, p_own, p_out, z_send, z_recv, f_send, f_recv,
    send_sems, recv_sems, local_sems,
):
    dp, tensor = lax.axis_index("dp"), lax.axis_index("tensor")
    x_hi, y, core = dp // 8, (dp // 2) % 4, dp % 2
    z, x_lo = tensor // 2, tensor % 2
    width = gate.shape[1]

    @functools.lru_cache(None)
    def dp_peer(rx, ry, rc):
        index = (((x_hi + rx) % 2) * 4 + (y + ry) % 4) * 2 + (core + rc) % 2
        return {"dp": index, "tensor": tensor}, index

    def z_peer(to):
        return {"dp": dp, "tensor": to * 2 + x_lo}

    @functools.lru_cache(None)
    def part_peer(j, r):
        pair, e = (z // 2 + 1 + j) % 4, (z + r) % 2
        return z_peer(pair * 2 + e), e

    @functools.lru_cache(None)
    def z_at(k):
        return (z + k) % 8

    x_peer = {"dp": dp, "tensor": z * 2 + 1 - x_lo}
    opposite = dp_peer(1, 0, 0)[0]
    above, below = dp_peer(0, 1, 0)[0], dp_peer(0, 3, 0)[0]
    twin = dp_peer(0, 0, 1)[0]

    copies = []

    def send(src, dst, peer):
        at = len(copies)
        copy = pltpu.make_async_remote_copy(
            src_ref=src, dst_ref=dst, send_sem=send_sems.at[at], recv_sem=recv_sems.at[at],
            device_id=peer, device_id_type=MESH,
        )
        copy.start()
        copies.append(copy)
        return copy

    local = []

    def load(src, dst):
        copy = pltpu.make_async_copy(src, dst, local_sems.at[len(local)])
        copy.start()
        local.append(copy)
        return copy

    @functools.lru_cache(None)
    def rows(j):
        return pl.ds(pl.multiple_of(((z // 2 + 1 + j) % PARTS) * 32, 32), 32)

    act_load = load(act_hbm, act.at[0])
    loads = []

    def load_part(j):
        loads.append([load(src.at[rows(j)], dst.at[rows(j)]) for src, dst in (
            (gate_hbm, gate), (up_hbm, up), (hidden_hbm, hidden))])

    load_part(0)
    barrier = pltpu.get_barrier_semaphore()
    peers = [dp_peer(rx, ry, 0)[0] for rx, ry in CHUNKS[1:]] + [twin]
    peers += [part_peer(j, r)[0] for j in range(PARTS) for r in range(2) if j < PARTS - 1 or r] + [x_peer]
    for peer in peers:
        pl.semaphore_signal(barrier, inc=1, device_id=peer, device_id_type=MESH)

    got = {}
    a_pairs = []

    def send_part(chunk, j, peer, to_chunk):
        at = rows(j)
        got[to_chunk, j] = send(grads.at[SLOT[chunk], 0, at], grads.at[SLOT[to_chunk], 0, at], peer)

    def to_twin(chunk):
        got["twin", chunk] = send(grads.at[SLOT[chunk], 0], grads.at[SLOT[chunk], 1], twin)

    def wait_parts(chunks, parts):
        for chunk in chunks:
            for j in parts:
                if (chunk, j) in got:
                    got.pop((chunk, j)).wait_recv()

    def own_part(j):
        for copy in loads[j]:
            copy.wait()
        gate_value = gate[rows(j), :].astype(F32)
        up_value = up[rows(j), :].astype(F32)
        upstream = hidden[rows(j), :].astype(F32)
        gate_sigmoid = jax.nn.sigmoid(gate_value)
        scaled = upstream * gate_sigmoid
        grads[0, 0, rows(j), 0:width] = (
            scaled * up_value * (1.0 + gate_value * (1.0 - gate_sigmoid))
        ).astype(BF16)
        grads[0, 0, rows(j), width:2 * width] = (scaled * gate_value).astype(BF16)
        if j == 0:
            pl.semaphore_wait(barrier, len(peers))
            act_load.wait()
            a_pairs.append(send(act.at[0], act.at[1], x_peer))
        if j % 2 == 0:
            send_part((0, 0), j, above, (0, 3))
        else:
            send_part((0, 0), j, below, (0, 1))
        send_part((0, 0), j, opposite, (1, 0))

    own_part(0)
    for j in range(1, PARTS):
        load_part(j)
    weight_loads = [load(wgate_hbm, weights.at[0]), load(wup_hbm, weights.at[1])]
    for j in range(1, PARTS):
        own_part(j)
    a_pairs[0].wait_recv()
    mine, other = act[0].astype(F32), act[1].astype(F32)
    both = jnp.concatenate((jnp.where(x_lo == 0, mine, other), jnp.where(x_lo == 0, other, mine)), axis=0)
    for chip in range(8):
        for rc in range(2):
            at = (chip * 2 + rc) * 256
            a_send[chip, (rc + core) % 2] = both[:, at:at + 256].astype(BF16)
    a_copies = []
    for rx, ry in CHUNKS[1:]:
        peer, index = dp_peer(rx, ry, 0)
        a_copies.append(send(a_send.at[index // 2], a_got.at[SLOT[rx, -ry % 4]], peer))
    a_got[0] = a_send[dp // 2]
    to_twin((0, 0))
    for copy in weight_loads:
        copy.wait()
    for half in range(2):
        weights_t[0, half] = weights[half].astype(F32).T.astype(BF16)
    w_copy = send(weights_t.at[0], weights_t.at[1], twin)

    def ig_product(units, base):
        for first in range(0, len(units), 8):
            some = units[first:first + 8]
            wait_parts_of(some)
            lhs = jnp.concatenate([grads[SLOT[chunk], 0, rows(j), :] for chunk, j in some], axis=0)
            at = pl.ds(base + first, len(some))
            for rc in range(2):
                term = jnp.dot(lhs[:, :width], weights_t[rc, 0], preferred_element_type=F32)
                term += jnp.dot(lhs[:, width:], weights_t[rc, 1], preferred_element_type=F32)
                term = term.reshape(len(some), 2, 2, 8, 256)
                low, high = term[:, :, 0], term[:, :, 1]
                here = at, slice(None), pl.ds(rc * 8, 8)
                p_own[here] = jnp.where(x_lo == 0, low, high)
                p_out[here] = jnp.where(x_lo == 0, high, low)
            p_send[at] = p_out[at].astype(BF16)

    def wait_parts_of(units):
        for chunk, j in units:
            wait_parts([chunk], [j])

    def ig_exchange(base, n):
        at = pl.ds(base, n)
        return send(p_send.at[at], p_recv.at[at], x_peer)

    z_copies = {}

    def ig_pair(copy, units, base, spans):
        copy.wait_recv()
        for at, (chunk, j) in enumerate(units):
            z_send[j, :, SLOT[chunk]] = (p_own[base + at] + p_recv[base + at].astype(F32)).astype(BF16)
        for first, n, parts in spans:
            for j in parts:
                for r in range(2):
                    if j == PARTS - 1 and r == 0:
                        continue
                    peer, e = part_peer(j, r)
                    at = pl.ds(first, n)
                    z_copies.setdefault((0, 0, 2, 2, 2, 5, 6, 6)[first], []).append(
                        send(z_send.at[j, e, at], z_recv.at[j, r, at], peer))

    f_copies = []

    def ig_final(chunks):
        first = SLOT[chunks[0]]
        for copy in z_copies.pop(first):
            copy.wait_recv()
        for at, (rx, ry) in enumerate(chunks):
            total_z = z_send[PARTS - 1, z % 2, first + at].astype(F32)
            for j in range(PARTS):
                for r in range(2):
                    if j < PARTS - 1 or r:
                        total_z += z_recv[j, r, first + at].astype(F32)
            if rx or ry:
                f_send[first + at] = total_z
                back = rx * 4 + -ry % 4
                f_copies.append(send(f_send.at[first + at], f_recv.at[back], dp_peer(rx, ry, 0)[0]))
            else:
                f_recv[0] = total_z

    every = range(PARTS)

    def on_even(j):
        wait_parts([(0, 3)], [j])
        send_part((0, 3), j, above, (0, 2))

    def on_odd(j):
        wait_parts([(0, 1)], [j])
        send_part((0, 1), j, below, (0, 2))

    def opposite_part(j, order):
        wait_parts([(1, 0)], [j])
        for peer, to_chunk in order:
            send_part((1, 0), j, peer, to_chunk)

    up_first = ((above, (1, 3)), (below, (1, 1)))

    ring = {}

    def ring_step(step):
        if step == 0:
            a_twin.wait_recv()
        for half in range(2):
            for way, peer, block in (
                ("right", z_peer(z_at(1)), z_at(8 - step)), ("left", z_peer(z_at(7)), z_at(step))):
                if (way, half) in ring:
                    ring.pop((way, half)).wait_recv()
                if step < 3 or (step == 3 and half == (way == "left")):
                    part = a_all.at[block, pl.ds(half * 4, 4)]
                    ring[way, half] = send(part, part, peer)

    def a_turn(at):
        block = jnp.concatenate([a_all[zz, at, rc] for rc in range(2) for zz in range(8)], axis=0)
        a_t[:, at * 256:(at + 1) * 256] = block.astype(F32).T.astype(BF16)

    sent = [0]

    def drain():
        for copy in copies[sent[0]:]:
            copy.wait_send()
        sent[0] = len(copies)

    on_even(0)
    on_odd(1)
    opposite_part(0, up_first)
    w_copy.wait_recv()
    near = [(CHUNKS[at], j) for at in (0, 1) for j in every] + [((0, 3), 0), ((0, 3), 2), ((0, 1), 1), ((0, 1), 3)]
    ig_product(near[:4], 0)
    on_even(2)
    opposite_part(1, up_first[::-1])
    on_odd(3)
    for copy in a_copies:
        copy.wait_recv()
    a_all[z, :, 0] = a_got[:, 0]
    a_twin = send(a_got.at[:, 1], a_all.at[z, :, 1], twin)
    opposite_part(2, up_first)
    ring_step(0)
    opposite_part(3, up_first)
    to_twin((1, 0))
    wait_parts([(1, 3)], [0])
    send_part((1, 3), 0, above, (1, 2))
    for j in (1, 3):
        send_part((0, 0), j, above, (0, 3))
    ig_product(near[4:], 4)
    near_copy = ig_exchange(0, 12)
    wait_parts([(1, 1)], [1])
    send_part((1, 1), 1, below, (1, 2))
    for j in (0, 2):
        send_part((0, 0), j, below, (0, 1))
    wait_parts([(0, 2)], [2])
    send_part((0, 2), 2, opposite, (1, 2))
    ring_step(1)
    wait_parts([(0, 2)], [3])
    send_part((0, 2), 3, opposite, (1, 2))
    middle = [(chunk, j) for chunk in CHUNKS[2:5] for j in range(2)]
    ig_product(middle, 12)
    middle_copy = ig_exchange(12, 6)
    ring_step(2)
    ig_pair(near_copy, near, 0, [(0, 2, every), (7, 1, (0, 2)), (6, 1, (1, 3))])
    later = [(chunk, j) for chunk in CHUNKS[2:5] for j in range(2, 4)]
    ig_product(later, 18)
    later_copy = ig_exchange(18, 6)
    for chunk in CHUNKS[2:5]:
        to_twin(chunk)
    ig_pair(middle_copy, middle, 12, [(2, 3, range(2))])
    ring_step(3)
    across = [((1, 2), j) for j in every]
    ig_product(across, 24)
    across_copy = ig_exchange(24, 4)
    to_twin((1, 2))
    ig_pair(later_copy, later, 18, [(2, 3, range(2, 4))])
    ig_final(CHUNKS[:2])
    far = [((0, 3), 1), ((0, 1), 0)]
    ig_product(far, 28)
    far_copy = ig_exchange(28, 2)
    ig_pair(across_copy, across, 24, [(5, 1, every)])
    last = [((0, 3), 3), ((0, 1), 2)]
    ig_product(last, 30)
    last_copy = ig_exchange(30, 2)
    to_twin((0, 3))
    to_twin((0, 1))
    ig_pair(far_copy, far, 28, [(7, 1, (1,)), (6, 1, (0,))])
    ring_step(4)
    for at in range(8):
        a_turn(at)
    ig_pair(last_copy, last, 30, [(7, 1, (3,)), (6, 1, (2,))])
    ig_final(CHUNKS[2:5])
    ig_final(CHUNKS[5:6])
    for chunk in CHUNKS[:6]:
        got.pop(("twin", chunk)).wait_recv()
    for half in range(2):
        cols = slice(half * width, (half + 1) * width)
        total[:, cols] = jnp.dot(
            a_t[:, 0:1536], grads[0:6, :, :, cols].reshape(1536, width), preferred_element_type=F32)
    ig_final(CHUNKS[6:])
    for chunk in CHUNKS[6:]:
        got.pop(("twin", chunk)).wait_recv()
    outs = []
    for half, out_hbm in enumerate((ggrad_hbm, ugrad_hbm)):
        cols = slice(half * width, (half + 1) * width)
        out_buf[half] = ((total[:, cols] + jnp.dot(
            a_t[:, 1536:2048], grads[6:8, :, :, cols].reshape(512, width), preferred_element_type=F32)
        ) * grad_scale).astype(BF16)
        outs.append(load(out_buf.at[half], out_hbm))
    drain()
    assert not got
    for copy in f_copies:
        copy.wait_recv()
    for index in range(16):
        rel = ((index // 8 + x_hi) % 2) * 4 + (index // 2 % 4 - y + 4) % 4
        at = pl.ds(pl.multiple_of(((index % 2 + core) % 2) * 8, 8), 8)
        igrad[:, index * 256:(index + 1) * 256] = f_recv[rel, at].astype(BF16)
    outs.append(load(igrad, igrad_hbm))
    for copy in outs:
        copy.wait()


def body(*args):
    activations, gate_pre, _, _, gate_weight, _ = args
    own_tokens, model = activations.shape
    rows, width = gate_weight.shape
    tokens = gate_pre.shape[0]
    n_dp = lax.axis_size("dp")
    hbm = pl.BlockSpec(memory_space=pltpu.HBM)
    results = pl.pallas_call(
        functools.partial(kernel, float(tokens * n_dp) ** (-0.5)),
        out_shape=(
            jax.ShapeDtypeStruct((own_tokens, model), BF16),
            jax.ShapeDtypeStruct((rows, width), BF16),
            jax.ShapeDtypeStruct((rows, width), BF16),
        ),
        in_specs=[hbm] * 6,
        out_specs=(hbm, hbm, hbm),
        scratch_shapes=[
            pltpu.VMEM((2, own_tokens, model), BF16),
            pltpu.VMEM((tokens, width), BF16),
            pltpu.VMEM((tokens, width), BF16),
            pltpu.VMEM((tokens, width), BF16),
            pltpu.VMEM((2, rows, width), BF16),
            pltpu.VMEM((2, 2, width, rows), BF16),
            pltpu.VMEM((8, 2, tokens, 2 * width), BF16),
            pltpu.VMEM((8, 2, 16, 256), BF16),
            pltpu.VMEM((8, 2, 16, 256), BF16),
            pltpu.VMEM((8, 8, 2, 16, 256), BF16),
            pltpu.VMEM((rows, tokens * n_dp), BF16),
            pltpu.VMEM((rows, 2 * width), F32),
            pltpu.VMEM((2, rows, width), BF16),
            pltpu.VMEM((own_tokens, model), BF16),
            pltpu.VMEM((32, 2, 16, 256), BF16),
            pltpu.VMEM((32, 2, 16, 256), BF16),
            pltpu.VMEM((32, 2, 16, 256), F32),
            pltpu.VMEM((32, 2, 16, 256), F32),
            pltpu.VMEM((PARTS, 2, 8, 16, 256), BF16),
            pltpu.VMEM((PARTS, 2, 8, 16, 256), BF16),
            pltpu.VMEM((8, 16, 256), F32),
            pltpu.VMEM((8, 16, 256), F32),
            pltpu.SemaphoreType.DMA((N_COPIES,)),
            pltpu.SemaphoreType.DMA((N_COPIES,)),
            pltpu.SemaphoreType.DMA((32,)),
        ],
        compiler_params=pltpu.CompilerParams(
            collective_id=0, has_side_effects=True, vmem_limit_bytes=62 * 2**20
        ),
        cost_estimate=pl.CostEstimate(flops=3_758_096_384, bytes_accessed=4_500_000, transcendentals=114_688),
    )(*args)
    return pl.pallas_call(
        place,
        out_shape=tuple(jax.ShapeDtypeStruct(r.shape, r.dtype) for r in results),
        in_specs=[hbm] * 3,
        out_specs=(hbm,) * 3,
        scratch_shapes=[pltpu.VMEM(r.shape, r.dtype) for r in results] + [pltpu.SemaphoreType.DMA((6,))],
    )(*results)


def place(a_in, b_in, c_in, a_out, b_out, c_out, a, b, c, sems):
    steps = ((b_in, b, b_out), (c_in, c, c_out), (a_in, a, a_out))
    copies = [pltpu.make_async_copy(src, mid, sems.at[at]) for at, (src, mid, _) in enumerate(steps)]
    for copy in copies:
        copy.start()
    outs = []
    for at, (_, mid, dst) in enumerate(steps):
        copies[at].wait()
        outs.append(pltpu.make_async_copy(mid, dst, sems.at[3 + at]))
        outs[at].start()
    for copy in outs:
        copy.wait()


def solution(mesh):
    in_specs = (
        P(("dp", "tensor"), None),
        P("dp", "tensor"),
        P("dp", "tensor"),
        P("dp", "tensor"),
        P("dp", "tensor"),
        P("dp", "tensor"),
    )
    out_specs = (P(("dp", "tensor"), None), P("dp", "tensor"), P("dp", "tensor"))
    return jax.shard_map(body, mesh=mesh, in_specs=in_specs, out_specs=out_specs, check_vma=False)
```

```python
import functools

import jax
import jax.numpy as jnp
from jax import lax
from jax.experimental import pallas as pl
from jax.experimental.pallas import tpu as pltpu
from jax.sharding import PartitionSpec as P

MESH = pl.DeviceIdType.MESH
BF16, F32 = jnp.bfloat16, jnp.float32
CHUNKS = ((0, 0), (1, 0), (0, 2), (1, 1), (1, 3), (1, 2), (0, 1), (0, 3))
SLOT = {chunk: at for at, chunk in enumerate(CHUNKS)}
PARTS = 4
N_COPIES = 112


def kernel(
    grad_scale,
    act_hbm, gate_hbm, up_hbm, hidden_hbm, wgate_hbm, wup_hbm,
    igrad_hbm, ggrad_hbm, ugrad_hbm,
    act, gate, up, hidden, weights, weights_t, grads,
    a_send, a_got, a_all, a_t, total, out_buf, igrad,
    p_send, p_recv, p_own, p_out, z_send, z_recv, f_send, f_recv,
    send_sems, recv_sems, local_sems,
):
    dp, tensor = lax.axis_index("dp"), lax.axis_index("tensor")
    x_hi, y, core = dp // 8, (dp // 2) % 4, dp % 2
    z, x_lo = tensor // 2, tensor % 2
    width = gate.shape[1]

    @functools.lru_cache(None)
    def dp_peer(rx, ry, rc):
        index = (((x_hi + rx) % 2) * 4 + (y + ry) % 4) * 2 + (core + rc) % 2
        return {"dp": index, "tensor": tensor}, index

    def z_peer(to):
        return {"dp": dp, "tensor": to * 2 + x_lo}

    @functools.lru_cache(None)
    def part_peer(j, r):
        pair, e = (z // 2 + 1 + j) % 4, (z + r) % 2
        return z_peer(pair * 2 + e), e

    @functools.lru_cache(None)
    def z_at(k):
        return (z + k) % 8

    x_peer = {"dp": dp, "tensor": z * 2 + 1 - x_lo}
    opposite = dp_peer(1, 0, 0)[0]
    above, below = dp_peer(0, 1, 0)[0], dp_peer(0, 3, 0)[0]
    twin = dp_peer(0, 0, 1)[0]

    copies = []

    def send(src, dst, peer):
        at = len(copies)
        copy = pltpu.make_async_remote_copy(
            src_ref=src, dst_ref=dst, send_sem=send_sems.at[at], recv_sem=recv_sems.at[at],
            device_id=peer, device_id_type=MESH,
        )
        copy.start()
        copies.append(copy)
        return copy

    local = []

    def load(src, dst):
        copy = pltpu.make_async_copy(src, dst, local_sems.at[len(local)])
        copy.start()
        local.append(copy)
        return copy

    @functools.lru_cache(None)
    def rows(j):
        return pl.ds(pl.multiple_of(((z // 2 + 1 + j) % PARTS) * 32, 32), 32)

    act_load = load(act_hbm, act.at[0])
    loads = []

    def load_part(j):
        loads.append([load(src.at[rows(j)], dst.at[rows(j)]) for src, dst in (
            (gate_hbm, gate), (up_hbm, up), (hidden_hbm, hidden))])

    load_part(0)
    barrier = pltpu.get_barrier_semaphore()
    peers = [dp_peer(rx, ry, 0)[0] for rx, ry in CHUNKS[1:]] + [twin]
    peers += [part_peer(j, r)[0] for j in range(PARTS) for r in range(2) if j < PARTS - 1 or r] + [x_peer]
    for peer in peers:
        pl.semaphore_signal(barrier, inc=1, device_id=peer, device_id_type=MESH)

    got = {}
    a_pairs = []

    def send_part(chunk, j, peer, to_chunk):
        at = rows(j)
        got[to_chunk, j] = send(grads.at[SLOT[chunk], 0, at], grads.at[SLOT[to_chunk], 0, at], peer)

    def to_twin(chunk):
        got["twin", chunk] = send(grads.at[SLOT[chunk], 0], grads.at[SLOT[chunk], 1], twin)

    def wait_parts(chunks, parts):
        for chunk in chunks:
            for j in parts:
                if (chunk, j) in got:
                    got.pop((chunk, j)).wait_recv()

    def own_part(j):
        for copy in loads[j]:
            copy.wait()
        gate_value = gate[rows(j), :].astype(F32)
        up_value = up[rows(j), :].astype(F32)
        upstream = hidden[rows(j), :].astype(F32)
        gate_sigmoid = jax.nn.sigmoid(gate_value)
        scaled = upstream * gate_sigmoid
        grads[0, 0, rows(j), 0:width] = (
            scaled * up_value * (1.0 + gate_value * (1.0 - gate_sigmoid))
        ).astype(BF16)
        grads[0, 0, rows(j), width:2 * width] = (scaled * gate_value).astype(BF16)
        if j == 0:
            pl.semaphore_wait(barrier, len(peers))
            act_load.wait()
            a_pairs.append(send(act.at[0], act.at[1], x_peer))
        if j % 2 == 0:
            send_part((0, 0), j, above, (0, 3))
        else:
            send_part((0, 0), j, below, (0, 1))
        send_part((0, 0), j, opposite, (1, 0))

    own_part(0)
    for j in range(1, PARTS):
        load_part(j)
    weight_loads = [load(wgate_hbm, weights.at[0]), load(wup_hbm, weights.at[1])]
    for j in range(1, PARTS):
        own_part(j)
    a_pairs[0].wait_recv()
    mine, other = act[0].astype(F32), act[1].astype(F32)
    both = jnp.concatenate((jnp.where(x_lo == 0, mine, other), jnp.where(x_lo == 0, other, mine)), axis=0)
    for chip in range(8):
        for rc in range(2):
            at = (chip * 2 + rc) * 256
            a_send[chip, (rc + core) % 2] = both[:, at:at + 256].astype(BF16)
    a_copies = []
    for rx, ry in CHUNKS[1:]:
        peer, index = dp_peer(rx, ry, 0)
        a_copies.append(send(a_send.at[index // 2], a_got.at[SLOT[rx, -ry % 4]], peer))
    a_got[0] = a_send[dp // 2]
    to_twin((0, 0))
    for copy in weight_loads:
        copy.wait()
    for half in range(2):
        weights_t[0, half] = weights[half].astype(F32).T.astype(BF16)
    w_copy = send(weights_t.at[0], weights_t.at[1], twin)

    def ig_product(units, base):
        for first in range(0, len(units), 8):
            some = units[first:first + 8]
            wait_parts_of(some)
            lhs = jnp.concatenate([grads[SLOT[chunk], 0, rows(j), :] for chunk, j in some], axis=0)
            at = pl.ds(base + first, len(some))
            for rc in range(2):
                term = jnp.dot(lhs[:, :width], weights_t[rc, 0], preferred_element_type=F32)
                term += jnp.dot(lhs[:, width:], weights_t[rc, 1], preferred_element_type=F32)
                term = term.reshape(len(some), 2, 2, 8, 256)
                low, high = term[:, :, 0], term[:, :, 1]
                here = at, slice(None), pl.ds(rc * 8, 8)
                p_own[here] = jnp.where(x_lo == 0, low, high)
                p_out[here] = jnp.where(x_lo == 0, high, low)
            p_send[at] = p_out[at].astype(BF16)

    def wait_parts_of(units):
        for chunk, j in units:
            wait_parts([chunk], [j])

    def ig_exchange(base, n):
        at = pl.ds(base, n)
        return send(p_send.at[at], p_recv.at[at], x_peer)

    z_copies = {}

    def ig_pair(copy, units, base, spans):
        copy.wait_recv()
        for at, (chunk, j) in enumerate(units):
            z_send[j, :, SLOT[chunk]] = (p_own[base + at] + p_recv[base + at].astype(F32)).astype(BF16)
        for first, n, parts in spans:
            for j in parts:
                for r in range(2):
                    if j == PARTS - 1 and r == 0:
                        continue
                    peer, e = part_peer(j, r)
                    at = pl.ds(first, n)
                    z_copies.setdefault((0, 0, 2, 2, 2, 5, 6, 6)[first], []).append(
                        send(z_send.at[j, e, at], z_recv.at[j, r, at], peer))

    f_copies = []

    def ig_final(chunks):
        first = SLOT[chunks[0]]
        for copy in z_copies.pop(first):
            copy.wait_recv()
        for at, (rx, ry) in enumerate(chunks):
            total_z = z_send[PARTS - 1, z % 2, first + at].astype(F32)
            for j in range(PARTS):
                for r in range(2):
                    if j < PARTS - 1 or r:
                        total_z += z_recv[j, r, first + at].astype(F32)
            if rx or ry:
                f_send[first + at] = total_z
                back = rx * 4 + -ry % 4
                f_copies.append(send(f_send.at[first + at], f_recv.at[back], dp_peer(rx, ry, 0)[0]))
            else:
                f_recv[0] = total_z

    every = range(PARTS)

    def on_even(j):
        wait_parts([(0, 3)], [j])
        send_part((0, 3), j, above, (0, 2))

    def on_odd(j):
        wait_parts([(0, 1)], [j])
        send_part((0, 1), j, below, (0, 2))

    def opposite_part(j, order):
        wait_parts([(1, 0)], [j])
        for peer, to_chunk in order:
            send_part((1, 0), j, peer, to_chunk)

    up_first = ((above, (1, 3)), (below, (1, 1)))

    ring = {}

    def ring_step(step):
        if step == 0:
            a_twin.wait_recv()
        for half in range(2):
            for way, peer, block in (
                ("right", z_peer(z_at(1)), z_at(8 - step)), ("left", z_peer(z_at(7)), z_at(step))):
                if (way, half) in ring:
                    ring.pop((way, half)).wait_recv()
                if step < 3 or (step == 3 and half == (way == "left")):
                    part = a_all.at[block, pl.ds(half * 4, 4)]
                    ring[way, half] = send(part, part, peer)

    def a_turn(at):
        block = jnp.concatenate([a_all[zz, at, rc] for rc in range(2) for zz in range(8)], axis=0)
        a_t[:, at * 256:(at + 1) * 256] = block.astype(F32).T.astype(BF16)

    sent = [0]

    def drain():
        for copy in copies[sent[0]:]:
            copy.wait_send()
        sent[0] = len(copies)

    on_even(0)
    on_odd(1)
    opposite_part(0, up_first)
    w_copy.wait_recv()
    near = [(CHUNKS[at], j) for at in (0, 1) for j in every] + [((0, 3), 0), ((0, 3), 2), ((0, 1), 1), ((0, 1), 3)]
    ig_product(near[:4], 0)
    on_even(2)
    opposite_part(1, up_first[::-1])
    on_odd(3)
    for copy in a_copies:
        copy.wait_recv()
    a_all[z, :, 0] = a_got[:, 0]
    a_twin = send(a_got.at[:, 1], a_all.at[z, :, 1], twin)
    opposite_part(2, up_first)
    ring_step(0)
    opposite_part(3, up_first)
    to_twin((1, 0))
    wait_parts([(1, 3)], [0])
    send_part((1, 3), 0, above, (1, 2))
    for j in (1, 3):
        send_part((0, 0), j, above, (0, 3))
    ig_product(near[4:], 4)
    near_copy = ig_exchange(0, 12)
    wait_parts([(1, 1)], [1])
    send_part((1, 1), 1, below, (1, 2))
    for j in (0, 2):
        send_part((0, 0), j, below, (0, 1))
    wait_parts([(0, 2)], [2])
    send_part((0, 2), 2, opposite, (1, 2))
    ring_step(1)
    wait_parts([(0, 2)], [3])
    send_part((0, 2), 3, opposite, (1, 2))
    middle = [(chunk, j) for chunk in CHUNKS[2:5] for j in range(2)]
    ig_product(middle, 12)
    middle_copy = ig_exchange(12, 6)
    ring_step(2)
    ig_pair(near_copy, near, 0, [(0, 2, every), (7, 1, (0, 2)), (6, 1, (1, 3))])
    later = [(chunk, j) for chunk in CHUNKS[2:5] for j in range(2, 4)]
    ig_product(later, 18)
    later_copy = ig_exchange(18, 6)
    for chunk in CHUNKS[2:5]:
        to_twin(chunk)
    ig_pair(middle_copy, middle, 12, [(2, 3, range(2))])
    ring_step(3)
    across = [((1, 2), j) for j in every]
    ig_product(across, 24)
    across_copy = ig_exchange(24, 4)
    to_twin((1, 2))
    ig_pair(later_copy, later, 18, [(2, 3, range(2, 4))])
    ig_final(CHUNKS[:2])
    far = [((0, 3), 1), ((0, 1), 0)]
    ig_product(far, 28)
    far_copy = ig_exchange(28, 2)
    ig_pair(across_copy, across, 24, [(5, 1, every)])
    last = [((0, 3), 3), ((0, 1), 2)]
    ig_product(last, 30)
    last_copy = ig_exchange(30, 2)
    to_twin((0, 3))
    to_twin((0, 1))
    ig_pair(far_copy, far, 28, [(7, 1, (1,)), (6, 1, (0,))])
    ring_step(4)
    for at in range(8):
        a_turn(at)
    ig_pair(last_copy, last, 30, [(7, 1, (3,)), (6, 1, (2,))])
    ig_final(CHUNKS[2:5])
    ig_final(CHUNKS[5:6])
    ig_final(CHUNKS[6:])
    for chunk in CHUNKS[:6]:
        got.pop(("twin", chunk)).wait_recv()
    for half in range(2):
        cols = slice(half * width, (half + 1) * width)
        total[:, cols] = jnp.dot(
            a_t[:, 0:1536], grads[0:6, :, :, cols].reshape(1536, width), preferred_element_type=F32)
    for chunk in CHUNKS[6:]:
        got.pop(("twin", chunk)).wait_recv()
    outs = []
    for half, out_hbm in enumerate((ggrad_hbm, ugrad_hbm)):
        cols = slice(half * width, (half + 1) * width)
        out_buf[half] = ((total[:, cols] + jnp.dot(
            a_t[:, 1536:2048], grads[6:8, :, :, cols].reshape(512, width), preferred_element_type=F32)
        ) * grad_scale).astype(BF16)
        outs.append(load(out_buf.at[half], out_hbm))
    drain()
    assert not got
    for copy in f_copies:
        copy.wait_recv()
    for index in range(16):
        rel = ((index // 8 + x_hi) % 2) * 4 + (index // 2 % 4 - y + 4) % 4
        at = pl.ds(pl.multiple_of(((index % 2 + core) % 2) * 8, 8), 8)
        igrad[:, index * 256:(index + 1) * 256] = f_recv[rel, at].astype(BF16)
    outs.append(load(igrad, igrad_hbm))
    for copy in outs:
        copy.wait()


def body(*args):
    activations, gate_pre, _, _, gate_weight, _ = args
    own_tokens, model = activations.shape
    rows, width = gate_weight.shape
    tokens = gate_pre.shape[0]
    n_dp = lax.axis_size("dp")
    hbm = pl.BlockSpec(memory_space=pltpu.HBM)
    results = pl.pallas_call(
        functools.partial(kernel, float(tokens * n_dp) ** (-0.5)),
        out_shape=(
            jax.ShapeDtypeStruct((own_tokens, model), BF16),
            jax.ShapeDtypeStruct((rows, width), BF16),
            jax.ShapeDtypeStruct((rows, width), BF16),
        ),
        in_specs=[hbm] * 6,
        out_specs=(hbm, hbm, hbm),
        scratch_shapes=[
            pltpu.VMEM((2, own_tokens, model), BF16),
            pltpu.VMEM((tokens, width), BF16),
            pltpu.VMEM((tokens, width), BF16),
            pltpu.VMEM((tokens, width), BF16),
            pltpu.VMEM((2, rows, width), BF16),
            pltpu.VMEM((2, 2, width, rows), BF16),
            pltpu.VMEM((8, 2, tokens, 2 * width), BF16),
            pltpu.VMEM((8, 2, 16, 256), BF16),
            pltpu.VMEM((8, 2, 16, 256), BF16),
            pltpu.VMEM((8, 8, 2, 16, 256), BF16),
            pltpu.VMEM((rows, tokens * n_dp), BF16),
            pltpu.VMEM((rows, 2 * width), F32),
            pltpu.VMEM((2, rows, width), BF16),
            pltpu.VMEM((own_tokens, model), BF16),
            pltpu.VMEM((32, 2, 16, 256), BF16),
            pltpu.VMEM((32, 2, 16, 256), BF16),
            pltpu.VMEM((32, 2, 16, 256), F32),
            pltpu.VMEM((32, 2, 16, 256), F32),
            pltpu.VMEM((PARTS, 2, 8, 16, 256), BF16),
            pltpu.VMEM((PARTS, 2, 8, 16, 256), BF16),
            pltpu.VMEM((8, 16, 256), F32),
            pltpu.VMEM((8, 16, 256), F32),
            pltpu.SemaphoreType.DMA((N_COPIES,)),
            pltpu.SemaphoreType.DMA((N_COPIES,)),
            pltpu.SemaphoreType.DMA((32,)),
        ],
        compiler_params=pltpu.CompilerParams(
            collective_id=0, has_side_effects=True, vmem_limit_bytes=62 * 2**20
        ),
        cost_estimate=pl.CostEstimate(flops=3_758_096_384, bytes_accessed=4_500_000, transcendentals=114_688),
    )(*args)
    return pl.pallas_call(
        place,
        out_shape=tuple(jax.ShapeDtypeStruct(r.shape, r.dtype) for r in results),
        in_specs=[hbm] * 3,
        out_specs=(hbm,) * 3,
        scratch_shapes=[pltpu.VMEM(r.shape, r.dtype) for r in results] + [pltpu.SemaphoreType.DMA((6,))],
    )(*results)


def place(a_in, b_in, c_in, a_out, b_out, c_out, a, b, c, sems):
    steps = ((b_in, b, b_out), (c_in, c, c_out), (a_in, a, a_out))
    copies = [pltpu.make_async_copy(src, mid, sems.at[at]) for at, (src, mid, _) in enumerate(steps)]
    for copy in copies:
        copy.start()
    outs = []
    for at, (_, mid, dst) in enumerate(steps):
        copies[at].wait()
        outs.append(pltpu.make_async_copy(mid, dst, sems.at[3 + at]))
        outs[at].start()
    for copy in outs:
        copy.wait()


def solution(mesh):
    in_specs = (
        P(("dp", "tensor"), None),
        P("dp", "tensor"),
        P("dp", "tensor"),
        P("dp", "tensor"),
        P("dp", "tensor"),
        P("dp", "tensor"),
    )
    out_specs = (P(("dp", "tensor"), None), P("dp", "tensor"), P("dp", "tensor"))
    return jax.shard_map(body, mesh=mesh, in_specs=in_specs, out_specs=out_specs, check_vma=False)
```

```python
import functools

import jax
import jax.numpy as jnp
from jax import lax
from jax.experimental import pallas as pl
from jax.experimental.pallas import tpu as pltpu
from jax.sharding import PartitionSpec as P

MESH = pl.DeviceIdType.MESH
BF16, F32 = jnp.bfloat16, jnp.float32
CHUNKS = ((0, 0), (1, 0), (0, 2), (1, 1), (1, 3), (1, 2), (0, 1), (0, 3))
SLOT = {chunk: at for at, chunk in enumerate(CHUNKS)}
PARTS = 4
N_COPIES = 112


def kernel(
    grad_scale,
    act_hbm, gate_hbm, up_hbm, hidden_hbm, wgate_hbm, wup_hbm,
    igrad_hbm, ggrad_hbm, ugrad_hbm,
    act, gate, up, hidden, weights, weights_t, grads,
    a_send, a_got, a_all, a_t, total, out_buf, igrad,
    p_send, p_recv, p_own, p_out, z_send, z_recv, f_send, f_recv,
    send_sems, recv_sems, local_sems,
):
    dp, tensor = lax.axis_index("dp"), lax.axis_index("tensor")
    x_hi, y, core = dp // 8, (dp // 2) % 4, dp % 2
    z, x_lo = tensor // 2, tensor % 2
    width = gate.shape[1]

    @functools.lru_cache(None)
    def dp_peer(rx, ry, rc):
        index = (((x_hi + rx) % 2) * 4 + (y + ry) % 4) * 2 + (core + rc) % 2
        return {"dp": index, "tensor": tensor}, index

    def z_peer(to):
        return {"dp": dp, "tensor": to * 2 + x_lo}

    @functools.lru_cache(None)
    def part_peer(j, r):
        pair, e = (z // 2 + 1 + j) % 4, (z + r) % 2
        return z_peer(pair * 2 + e), e

    @functools.lru_cache(None)
    def z_at(k):
        return (z + k) % 8

    x_peer = {"dp": dp, "tensor": z * 2 + 1 - x_lo}
    opposite = dp_peer(1, 0, 0)[0]
    above, below = dp_peer(0, 1, 0)[0], dp_peer(0, 3, 0)[0]
    twin = dp_peer(0, 0, 1)[0]

    copies = []

    def send(src, dst, peer):
        at = len(copies)
        copy = pltpu.make_async_remote_copy(
            src_ref=src, dst_ref=dst, send_sem=send_sems.at[at], recv_sem=recv_sems.at[at],
            device_id=peer, device_id_type=MESH,
        )
        copy.start()
        copies.append(copy)
        return copy

    local = []

    def load(src, dst):
        copy = pltpu.make_async_copy(src, dst, local_sems.at[len(local)])
        copy.start()
        local.append(copy)
        return copy

    @functools.lru_cache(None)
    def rows(j):
        return pl.ds(pl.multiple_of(((z // 2 + 1 + j) % PARTS) * 32, 32), 32)

    act_load = load(act_hbm, act.at[0])
    loads = []

    def load_part(j):
        loads.append([load(src.at[rows(j)], dst.at[rows(j)]) for src, dst in (
            (gate_hbm, gate), (up_hbm, up), (hidden_hbm, hidden))])

    load_part(0)
    barrier = pltpu.get_barrier_semaphore()
    peers = [dp_peer(rx, ry, 0)[0] for rx, ry in CHUNKS[1:]] + [twin]
    peers += [part_peer(j, r)[0] for j in range(PARTS) for r in range(2) if j < PARTS - 1 or r] + [x_peer]
    for peer in peers:
        pl.semaphore_signal(barrier, inc=1, device_id=peer, device_id_type=MESH)

    got = {}
    a_pairs = []

    def send_part(chunk, j, peer, to_chunk):
        at = rows(j)
        got[to_chunk, j] = send(grads.at[SLOT[chunk], 0, at], grads.at[SLOT[to_chunk], 0, at], peer)

    def to_twin(chunk):
        got["twin", chunk] = send(grads.at[SLOT[chunk], 0], grads.at[SLOT[chunk], 1], twin)

    def wait_parts(chunks, parts):
        for chunk in chunks:
            for j in parts:
                if (chunk, j) in got:
                    got.pop((chunk, j)).wait_recv()

    def own_part(j):
        for copy in loads[j]:
            copy.wait()
        gate_value = gate[rows(j), :].astype(F32)
        up_value = up[rows(j), :].astype(F32)
        upstream = hidden[rows(j), :].astype(F32)
        gate_sigmoid = jax.nn.sigmoid(gate_value)
        scaled = upstream * gate_sigmoid
        grads[0, 0, rows(j), 0:width] = (
            scaled * up_value * (1.0 + gate_value * (1.0 - gate_sigmoid))
        ).astype(BF16)
        grads[0, 0, rows(j), width:2 * width] = (scaled * gate_value).astype(BF16)
        if j == 0:
            pl.semaphore_wait(barrier, len(peers))
            act_load.wait()
            a_pairs.append(send(act.at[0], act.at[1], x_peer))
        if j % 2 == 0:
            send_part((0, 0), j, above, (0, 3))
        else:
            send_part((0, 0), j, below, (0, 1))
        send_part((0, 0), j, opposite, (1, 0))

    own_part(0)
    for j in range(1, PARTS):
        load_part(j)
    weight_loads = [load(wgate_hbm, weights.at[0]), load(wup_hbm, weights.at[1])]
    for j in range(1, PARTS):
        own_part(j)
    a_pairs[0].wait_recv()
    mine, other = act[0].astype(F32), act[1].astype(F32)
    both = jnp.concatenate((jnp.where(x_lo == 0, mine, other), jnp.where(x_lo == 0, other, mine)), axis=0)
    for chip in range(8):
        for rc in range(2):
            at = (chip * 2 + rc) * 256
            a_send[chip, (rc + core) % 2] = both[:, at:at + 256].astype(BF16)
    a_copies = []
    for rx, ry in CHUNKS[1:]:
        peer, index = dp_peer(rx, ry, 0)
        a_copies.append(send(a_send.at[index // 2], a_got.at[SLOT[rx, -ry % 4]], peer))
    a_got[0] = a_send[dp // 2]
    to_twin((0, 0))
    for copy in weight_loads:
        copy.wait()
    for half in range(2):
        weights_t[0, half] = weights[half].astype(F32).T.astype(BF16)
    w_copy = send(weights_t.at[0], weights_t.at[1], twin)

    def ig_product(units, base):
        for first in range(0, len(units), 8):
            some = units[first:first + 8]
            wait_parts_of(some)
            lhs = jnp.concatenate([grads[SLOT[chunk], 0, rows(j), :] for chunk, j in some], axis=0)
            at = pl.ds(base + first, len(some))
            for rc in range(2):
                term = jnp.dot(lhs[:, :width], weights_t[rc, 0], preferred_element_type=F32)
                term += jnp.dot(lhs[:, width:], weights_t[rc, 1], preferred_element_type=F32)
                term = term.reshape(len(some), 2, 2, 8, 256)
                low, high = term[:, :, 0], term[:, :, 1]
                here = at, slice(None), pl.ds(rc * 8, 8)
                p_own[here] = jnp.where(x_lo == 0, low, high)
                p_out[here] = jnp.where(x_lo == 0, high, low)
            p_send[at] = p_out[at].astype(BF16)

    def wait_parts_of(units):
        for chunk, j in units:
            wait_parts([chunk], [j])

    def ig_exchange(base, n):
        at = pl.ds(base, n)
        return send(p_send.at[at], p_recv.at[at], x_peer)

    z_copies = {}

    def ig_pair(copy, units, base, spans):
        copy.wait_recv()
        for at, (chunk, j) in enumerate(units):
            z_send[j, :, SLOT[chunk]] = (p_own[base + at] + p_recv[base + at].astype(F32)).astype(BF16)
        for first, n, parts in spans:
            for j in parts:
                for r in range(2):
                    if j == PARTS - 1 and r == 0:
                        continue
                    peer, e = part_peer(j, r)
                    at = pl.ds(first, n)
                    z_copies.setdefault((0, 0, 2, 2, 2, 5, 6, 6)[first], []).append(
                        send(z_send.at[j, e, at], z_recv.at[j, r, at], peer))

    f_copies = []

    def ig_final(chunks):
        first = SLOT[chunks[0]]
        for copy in z_copies.pop(first):
            copy.wait_recv()
        for at, (rx, ry) in enumerate(chunks):
            total_z = z_send[PARTS - 1, z % 2, first + at].astype(F32)
            for j in range(PARTS):
                for r in range(2):
                    if j < PARTS - 1 or r:
                        total_z += z_recv[j, r, first + at].astype(F32)
            if rx or ry:
                f_send[first + at] = total_z
                back = rx * 4 + -ry % 4
                f_copies.append(send(f_send.at[first + at], f_recv.at[back], dp_peer(rx, ry, 0)[0]))
            else:
                f_recv[0] = total_z

    every = range(PARTS)

    def on_even(j):
        wait_parts([(0, 3)], [j])
        send_part((0, 3), j, above, (0, 2))

    def on_odd(j):
        wait_parts([(0, 1)], [j])
        send_part((0, 1), j, below, (0, 2))

    def opposite_part(j, order):
        wait_parts([(1, 0)], [j])
        for peer, to_chunk in order:
            send_part((1, 0), j, peer, to_chunk)

    up_first = ((above, (1, 3)), (below, (1, 1)))

    ring = {}

    def ring_step(step):
        if step == 0:
            a_twin.wait_recv()
        for half in range(2):
            for way, peer, block in (
                ("right", z_peer(z_at(1)), z_at(8 - step)), ("left", z_peer(z_at(7)), z_at(step))):
                if (way, half) in ring:
                    ring.pop((way, half)).wait_recv()
                if step < 3 or (step == 3 and half == (way == "left")):
                    part = a_all.at[block, pl.ds(half * 4, 4)]
                    ring[way, half] = send(part, part, peer)

    def a_turn(at):
        block = jnp.concatenate([a_all[zz, at, rc] for rc in range(2) for zz in range(8)], axis=0)
        a_t[:, at * 256:(at + 1) * 256] = block.astype(F32).T.astype(BF16)

    sent = [0]

    def drain(upto):
        for copy in copies[sent[0]:upto]:
            copy.wait_send()
        sent[0] = upto

    on_even(0)
    on_odd(1)
    opposite_part(0, up_first)
    w_copy.wait_recv()
    near = [(CHUNKS[at], j) for at in (0, 1) for j in every] + [((0, 3), 0), ((0, 3), 2), ((0, 1), 1), ((0, 1), 3)]
    ig_product(near[:4], 0)
    on_even(2)
    opposite_part(1, up_first[::-1])
    on_odd(3)
    for copy in a_copies:
        copy.wait_recv()
    a_all[z, :, 0] = a_got[:, 0]
    a_twin = send(a_got.at[:, 1], a_all.at[z, :, 1], twin)
    opposite_part(2, up_first)
    ring_step(0)
    opposite_part(3, up_first)
    to_twin((1, 0))
    wait_parts([(1, 3)], [0])
    send_part((1, 3), 0, above, (1, 2))
    for j in (1, 3):
        send_part((0, 0), j, above, (0, 3))
    ig_product(near[4:], 4)
    near_copy = ig_exchange(0, 12)
    wait_parts([(1, 1)], [1])
    send_part((1, 1), 1, below, (1, 2))
    for j in (0, 2):
        send_part((0, 0), j, below, (0, 1))
    wait_parts([(0, 2)], [2])
    send_part((0, 2), 2, opposite, (1, 2))
    ring_step(1)
    wait_parts([(0, 2)], [3])
    send_part((0, 2), 3, opposite, (1, 2))
    middle = [(chunk, j) for chunk in CHUNKS[2:5] for j in range(2)]
    ig_product(middle, 12)
    middle_copy = ig_exchange(12, 6)
    ring_step(2)
    ig_pair(near_copy, near, 0, [(0, 2, every), (7, 1, (0, 2)), (6, 1, (1, 3))])
    later = [(chunk, j) for chunk in CHUNKS[2:5] for j in range(2, 4)]
    ig_product(later, 18)
    later_copy = ig_exchange(18, 6)
    for chunk in CHUNKS[2:5]:
        to_twin(chunk)
    ig_pair(middle_copy, middle, 12, [(2, 3, range(2))])
    ring_step(3)
    across = [((1, 2), j) for j in every]
    ig_product(across, 24)
    across_copy = ig_exchange(24, 4)
    to_twin((1, 2))
    ig_pair(later_copy, later, 18, [(2, 3, range(2, 4))])
    ig_final(CHUNKS[:2])
    far = [((0, 3), 1), ((0, 1), 0)]
    ig_product(far, 28)
    far_copy = ig_exchange(28, 2)
    ig_pair(across_copy, across, 24, [(5, 1, every)])
    last = [((0, 3), 3), ((0, 1), 2)]
    ig_product(last, 30)
    last_copy = ig_exchange(30, 2)
    to_twin((0, 3))
    to_twin((0, 1))
    ig_pair(far_copy, far, 28, [(7, 1, (1,)), (6, 1, (0,))])
    ring_step(4)
    for at in range(8):
        a_turn(at)
    ig_pair(last_copy, last, 30, [(7, 1, (3,)), (6, 1, (2,))])
    ig_final(CHUNKS[2:5])
    ig_final(CHUNKS[5:6])
    ig_final(CHUNKS[6:])
    for chunk in CHUNKS[:6]:
        got.pop(("twin", chunk)).wait_recv()
    for half in range(2):
        cols = slice(half * width, (half + 1) * width)
        total[:, cols] = jnp.dot(
            a_t[:, 0:1536], grads[0:6, :, :, cols].reshape(1536, width), preferred_element_type=F32)
    for chunk in CHUNKS[6:]:
        got.pop(("twin", chunk)).wait_recv()
    outs = []
    for half, out_hbm in enumerate((ggrad_hbm, ugrad_hbm)):
        cols = slice(half * width, (half + 1) * width)
        out_buf[half] = ((total[:, cols] + jnp.dot(
            a_t[:, 1536:2048], grads[6:8, :, :, cols].reshape(512, width), preferred_element_type=F32)
        ) * grad_scale).astype(BF16)
        outs.append(load(out_buf.at[half], out_hbm))
    drain(len(copies) // 2)
    assert not got
    for copy in f_copies:
        copy.wait_recv()
    for index in range(16):
        rel = ((index // 8 + x_hi) % 2) * 4 + (index // 2 % 4 - y + 4) % 4
        at = pl.ds(pl.multiple_of(((index % 2 + core) % 2) * 8, 8), 8)
        igrad[:, index * 256:(index + 1) * 256] = f_recv[rel, at].astype(BF16)
    outs.append(load(igrad, igrad_hbm))
    drain(len(copies))
    for copy in outs:
        copy.wait()


def body(*args):
    activations, gate_pre, _, _, gate_weight, _ = args
    own_tokens, model = activations.shape
    rows, width = gate_weight.shape
    tokens = gate_pre.shape[0]
    n_dp = lax.axis_size("dp")
    hbm = pl.BlockSpec(memory_space=pltpu.HBM)
    results = pl.pallas_call(
        functools.partial(kernel, float(tokens * n_dp) ** (-0.5)),
        out_shape=(
            jax.ShapeDtypeStruct((own_tokens, model), BF16),
            jax.ShapeDtypeStruct((rows, width), BF16),
            jax.ShapeDtypeStruct((rows, width), BF16),
        ),
        in_specs=[hbm] * 6,
        out_specs=(hbm, hbm, hbm),
        scratch_shapes=[
            pltpu.VMEM((2, own_tokens, model), BF16),
            pltpu.VMEM((tokens, width), BF16),
            pltpu.VMEM((tokens, width), BF16),
            pltpu.VMEM((tokens, width), BF16),
            pltpu.VMEM((2, rows, width), BF16),
            pltpu.VMEM((2, 2, width, rows), BF16),
            pltpu.VMEM((8, 2, tokens, 2 * width), BF16),
            pltpu.VMEM((8, 2, 16, 256), BF16),
            pltpu.VMEM((8, 2, 16, 256), BF16),
            pltpu.VMEM((8, 8, 2, 16, 256), BF16),
            pltpu.VMEM((rows, tokens * n_dp), BF16),
            pltpu.VMEM((rows, 2 * width), F32),
            pltpu.VMEM((2, rows, width), BF16),
            pltpu.VMEM((own_tokens, model), BF16),
            pltpu.VMEM((32, 2, 16, 256), BF16),
            pltpu.VMEM((32, 2, 16, 256), BF16),
            pltpu.VMEM((32, 2, 16, 256), F32),
            pltpu.VMEM((32, 2, 16, 256), F32),
            pltpu.VMEM((PARTS, 2, 8, 16, 256), BF16),
            pltpu.VMEM((PARTS, 2, 8, 16, 256), BF16),
            pltpu.VMEM((8, 16, 256), F32),
            pltpu.VMEM((8, 16, 256), F32),
            pltpu.SemaphoreType.DMA((N_COPIES,)),
            pltpu.SemaphoreType.DMA((N_COPIES,)),
            pltpu.SemaphoreType.DMA((32,)),
        ],
        compiler_params=pltpu.CompilerParams(
            collective_id=0, has_side_effects=True, vmem_limit_bytes=62 * 2**20
        ),
        cost_estimate=pl.CostEstimate(flops=3_758_096_384, bytes_accessed=4_500_000, transcendentals=114_688),
    )(*args)
    return pl.pallas_call(
        place,
        out_shape=tuple(jax.ShapeDtypeStruct(r.shape, r.dtype) for r in results),
        in_specs=[hbm] * 3,
        out_specs=(hbm,) * 3,
        scratch_shapes=[pltpu.VMEM(r.shape, r.dtype) for r in results] + [pltpu.SemaphoreType.DMA((6,))],
    )(*results)


def place(a_in, b_in, c_in, a_out, b_out, c_out, a, b, c, sems):
    steps = ((b_in, b, b_out), (c_in, c, c_out), (a_in, a, a_out))
    copies = [pltpu.make_async_copy(src, mid, sems.at[at]) for at, (src, mid, _) in enumerate(steps)]
    for copy in copies:
        copy.start()
    outs = []
    for at, (_, mid, dst) in enumerate(steps):
        copies[at].wait()
        outs.append(pltpu.make_async_copy(mid, dst, sems.at[3 + at]))
        outs[at].start()
    for copy in outs:
        copy.wait()


def solution(mesh):
    in_specs = (
        P(("dp", "tensor"), None),
        P("dp", "tensor"),
        P("dp", "tensor"),
        P("dp", "tensor"),
        P("dp", "tensor"),
        P("dp", "tensor"),
    )
    out_specs = (P(("dp", "tensor"), None), P("dp", "tensor"), P("dp", "tensor"))
    return jax.shard_map(body, mesh=mesh, in_specs=in_specs, out_specs=out_specs, check_vma=False)
```
